32 devices in a mesh: energy: 16 (over z, y, x), slab: 2 (over core).
Axes of the slice: x: 2, y: 2, z: 4, core: 2. Of those that a mesh axis runs over, the one named last changes fastest.
Arguments:
- onsite: float32 [2, 256, 256], P('slab')
- hopping: float32 [2, 256, 256], P('slab')
- sigma_less: float32 [16, 2, 256, 256], P('energy', 'slab')
- sigma_great: float32 [16, 2, 256, 256], P('energy', 'slab')
- phonon_shift: int32 [1], replicated, may hold values from 1 to 7
- occupation: float32 [1], replicated, may hold values from 0.3 to 3
Outputs:
- new_less: float32 [16, 2, 256, 256], P('energy', 'slab')
- new_great: float32 [16, 2, 256, 256], P('energy', 'slab')
The draws below stay inside these ranges and needn't reach their ends.
All inputs are finite; a program needn't handle non-finite values.
Results may differ from the reference program's by a relative error of at most 0.00015.
Values sent between devices are 32-bit elements; how exact they have to be, the bound alone decides.
A program may use at most 64 MiB of HBM per device.

```python
import math
import jax
import jax.numpy as jnp
from jax import lax

ORB = 256
OFFSET_BITS = 4
ENERGIES = 16
SLABS = 2


def slab_scales(key):
    return jnp.exp(jax.random.uniform(jax.random.fold_in(key, 5), (SLABS, ORB), jnp.float32, 0.0, math.log(2.0)))


def symmetric_blocks(key, block_count, dimension, middle, off_reach):
    scatter = jax.random.uniform(key, (block_count, dimension, dimension), jnp.float32, -off_reach, off_reach)
    scatter = 0.5 * (scatter + jnp.swapaxes(scatter, 1, 2))
    return jnp.where(jnp.eye(dimension, dtype=bool), middle[:, :, None], scatter)


def draw_onsite(key, part):
    scales = slab_scales(key)
    return symmetric_blocks(jax.random.fold_in(key, 11), SLABS, ORB, scales, 0.5 / ORB)


def draw_hopping(key, part):
    scales = slab_scales(key)
    previous = jnp.concatenate([jnp.ones((1, ORB), jnp.float32), scales[:-1]], 0)
    middle = 0.5 * jnp.sqrt(scales * previous)
    reach = 0.06 / math.sqrt(ORB)
    dense = jax.random.uniform(jax.random.fold_in(key, 17), (SLABS, ORB, ORB), jnp.float32, -reach, reach)
    return jnp.where(jnp.eye(ORB, dtype=bool), middle[:, :, None], dense)


def sigma_blocks(key):
    highest = 0.3
    middle = jnp.exp(jax.random.uniform(jax.random.fold_in(key, 3), (ENERGIES * SLABS, ORB), jnp.float32, math.log(0.05), math.log(highest)))
    blocks = symmetric_blocks(jax.random.fold_in(key, 7), ENERGIES * SLABS, ORB, middle, 0.4 / ORB)
    return blocks.reshape(ENERGIES, SLABS, ORB, ORB)


def draw_sigma_less(key, part):
    return sigma_blocks(jax.random.fold_in(key, 23))


def draw_sigma_great(key, part):
    return sigma_blocks(jax.random.fold_in(key, 37))


def setup_inputs(seed: int = 0) -> dict:
    key_list = jax.random.split(jax.random.key(seed), 7)
    onsite = draw_onsite(jax.random.fold_in(key_list[6], 71), 0)
    hopping = draw_hopping(jax.random.fold_in(key_list[6], 71), 0)
    sigma_less = draw_sigma_less(jax.random.fold_in(key_list[6], 71), 0)
    sigma_great = draw_sigma_great(jax.random.fold_in(key_list[6], 71), 0)
    phonon_shift = jax.random.randint(key_list[4], (1,), 1, min(2 ** OFFSET_BITS, ENERGIES // 2)).astype(jnp.int32)
    occupation = jnp.clip(jax.random.uniform(key_list[5], (1,), jnp.float32, 0.3, 3.0), 0.3, 3.0)
    return {"onsite": onsite, "hopping": hopping, "sigma_less": sigma_less, "sigma_great": sigma_great, "phonon_shift": phonon_shift, "occupation": occupation}


def matmul_high(first_matrix, second_matrix):
    return jnp.matmul(first_matrix, second_matrix, precision=lax.Precision.HIGHEST)

def swap_last(matrix):
    return jnp.swapaxes(matrix, -1, -2)

def invert_definite(matrix):
    factor = jnp.linalg.cholesky(matrix)
    identity = jnp.eye(matrix.shape[-1], dtype=matrix.dtype)

    def solve_one(factor_one):
        return jax.scipy.linalg.solve_triangular(factor_one, identity, lower=True)
    inverse_factor = jax.vmap(solve_one)(factor)
    return matmul_high(swap_last(inverse_factor), inverse_factor)

def forward_slab(block, coupling, source_less, source_great, green_left, less_left, great_left):
    coupled = matmul_high(swap_last(coupling), matmul_high(green_left, coupling))
    inverse = invert_definite(block - coupled)
    inner_less = source_less + matmul_high(swap_last(coupling), matmul_high(less_left, coupling))
    inner_great = source_great + matmul_high(swap_last(coupling), matmul_high(great_left, coupling))
    return (inverse, matmul_high(matmul_high(inverse, inner_less), inverse), matmul_high(matmul_high(inverse, inner_great), inverse))

def backward_slab(green_left, less_left, great_left, right_green, right_less, right_great):
    spread = matmul_high(green_left, right_green)
    green_full = green_left + matmul_high(spread, green_left)
    cross_less = matmul_high(spread, less_left)
    less_full = less_left + matmul_high(matmul_high(green_left, right_less), green_left) + cross_less + swap_last(cross_less)
    cross_great = matmul_high(spread, great_left)
    great_full = great_left + matmul_high(matmul_high(green_left, right_great), green_left) + cross_great + swap_last(cross_great)
    return (green_full, less_full, great_full)

def project(coupling, matrix):
    return matmul_high(matmul_high(coupling, matrix), swap_last(coupling))

def reference(onsite, hopping, sigma_less, sigma_great, phonon_shift, occupation):
    energy_total = sigma_less.shape[0]
    slab_total = sigma_less.shape[1]
    orbitals = sigma_less.shape[2]
    identity = jnp.eye(orbitals, dtype=jnp.float32)
    shift_values = 0.05 + 0.2 * jnp.arange(energy_total).astype(jnp.float32) / energy_total
    green_left = jnp.broadcast_to(identity, (energy_total, orbitals, orbitals))
    less_left = jnp.zeros((energy_total, orbitals, orbitals), jnp.float32)
    great_left = jnp.zeros((energy_total, orbitals, orbitals), jnp.float32)
    left_list = []
    for slab_pos in range(slab_total):
        block = onsite[slab_pos] + shift_values[:, None, None] * identity + 0.5 * (sigma_less[:, slab_pos] + sigma_great[:, slab_pos])
        green_left, less_left, great_left = forward_slab(block, hopping[slab_pos], sigma_less[:, slab_pos], sigma_great[:, slab_pos], green_left, less_left, great_left)
        left_list.append((green_left, less_left, great_left))
    right_green = jnp.zeros((energy_total, orbitals, orbitals), jnp.float32)
    right_less = jnp.zeros((energy_total, orbitals, orbitals), jnp.float32)
    right_great = jnp.zeros((energy_total, orbitals, orbitals), jnp.float32)
    less_list = [None] * slab_total
    great_list = [None] * slab_total
    for slab_pos in reversed(range(slab_total)):
        green_here, less_here, great_here = left_list[slab_pos]
        green_full, less_full, great_full = backward_slab(green_here, less_here, great_here, right_green, right_less, right_great)
        less_list[slab_pos] = less_full
        great_list[slab_pos] = great_full
        right_green = project(hopping[slab_pos], green_full)
        right_less = project(hopping[slab_pos], less_full)
        right_great = project(hopping[slab_pos], great_full)
    full_less = jnp.stack(less_list, 1)
    full_great = jnp.stack(great_list, 1)
    offset = phonon_shift[0].astype(jnp.int32)
    occupancy = occupation[0]

    def shifted(values):
        zero_pad = jnp.zeros_like(values)
        from_above = lax.dynamic_slice_in_dim(jnp.concatenate([values, zero_pad], 0), offset, energy_total, 0)
        from_below = lax.dynamic_slice_in_dim(jnp.concatenate([zero_pad, values], 0), (energy_total - offset).astype(jnp.int32), energy_total, 0)
        return (from_above, from_below)
    less_above, less_below = shifted(full_less)
    great_above, great_below = shifted(full_great)
    new_less = (occupancy + 1.0) * less_above + occupancy * less_below
    new_great = (occupancy + 1.0) * great_below + occupancy * great_above
    return (new_less, new_great)
```

```python
import functools
import jax
import jax.numpy as jnp
from jax import lax
from jax.experimental import pallas as pl
from jax.experimental.pallas import tpu as pltpu
from jax.sharding import PartitionSpec as P

OFFSET_BITS = 4


def split(matrix):
    high = matrix.astype(jnp.bfloat16)
    return high, (matrix - high.astype(jnp.float32)).astype(jnp.bfloat16)


def dot_pass(first, second, transposed):
    contract = (((1,), (1 if transposed else 0,)), ((), ()))
    return lax.dot_general(first, second, contract, preferred_element_type=jnp.float32)


def dot3(first, second, transposed=False):
    small = dot_pass(first[0], second[1], transposed) + dot_pass(first[1], second[0], transposed)
    return dot_pass(first[0], second[0], transposed) + small


def unit_matrix(orbitals):
    rows = lax.broadcasted_iota(jnp.int32, (orbitals, orbitals), 0)
    columns = lax.broadcasted_iota(jnp.int32, (orbitals, orbitals), 1)
    return rows == columns


def invert_definite(matrix, x_ref):
    orbitals = matrix.shape[0]
    on_diagonal = unit_matrix(orbitals)
    matrix = 0.5 * (matrix + matrix.T)
    diagonal = jnp.where(on_diagonal, matrix, 0.0)
    scale = lax.rsqrt(jnp.sum(diagonal, 0, keepdims=True)) * lax.rsqrt(jnp.sum(diagonal, 1, keepdims=True))
    scaled = matrix * scale
    reach = jnp.max(jnp.sum(jnp.abs(scaled), 1, keepdims=True))
    weight = jnp.minimum(1.0, 1.96 / reach)
    x_ref[...] = jnp.where(on_diagonal, 2.0 * weight, 0.0) - (weight * weight) * scaled
    scaled_parts = split(scaled)

    def going_on(state):
        step, residual = state
        return jnp.logical_and(step < 60, residual > 4e-6)

    def refine(state):
        step, _ = state
        x_parts = split(x_ref[...])
        gap = jnp.where(on_diagonal, 1.0, 0.0) - dot3(scaled_parts, x_parts)
        x_ref[...] += dot3(x_parts, split(gap))
        return step + 1, jnp.sum(gap * gap)

    lax.while_loop(going_on, refine, (jnp.int32(0), jnp.float32(1.0)))
    return x_ref[...] * scale


def recursion_kernel(n_slab, n_energy, *refs):
    own_and_others = refs[: 4 * n_slab]
    out_ref, x_ref, arrays = refs[4 * n_slab :]
    slab_index = lax.axis_index("slab")
    energy = lax.axis_index("energy").astype(jnp.float32)
    orbitals = x_ref.shape[0]
    for distance in range(n_slab):
        place = lax.rem(slab_index + distance, n_slab)
        for kind in range(4):
            arrays[kind, place] = own_and_others[distance * 4 + kind][...]
    shift = jnp.where(unit_matrix(orbitals), 0.05 + 0.2 * energy / n_energy, 0.0)
    greens, inners, spreads = [], [], []
    for i in range(n_slab):
        coupling = arrays[1, i]
        coupling_t = split(coupling.T)
        sources = [arrays[2, i], arrays[3, i]]
        block = arrays[0, i] + shift + 0.5 * (sources[0] + sources[1])
        if i == 0:
            coupled = dot3(coupling_t, split(coupling))
        else:
            spread = dot3(greens[-1], split(coupling))
            spread_parts = split(spread)
            coupled = dot3(coupling_t, spread_parts)
            spread_t = split(spread.T)
            sources = [
                source + dot3(spread_t, split(dot3(split(inner), spread_parts)))
                for source, inner in zip(sources, inners[-1])
            ]
            spreads.append(spread_parts)
        greens.append(split(invert_definite(block - coupled, x_ref)))
        inners.append(sources)

    green_full = greens[-1]
    full = [dot3(split(dot3(greens[-1], split(inner))), greens[-1]) for inner in inners[-1]]

    @pl.when(slab_index == n_slab - 1)
    def _():
        for kind in range(2):
            out_ref[kind] = full[kind]

    @pl.when(slab_index < n_slab - 1)
    def _():
        full_here, green_here = full, green_full
        for i in reversed(range(n_slab - 1)):
            green, spread = greens[i], spreads[i]
            extra = dot3(split(dot3(spread, green_here)), spread, True)
            extra_parts = split(extra)
            parts = []
            for kind in range(2):
                half = split(dot3(split(inners[i][kind]), green))
                cross = dot3(extra_parts, half)
                passed = dot3(split(dot3(spread, split(full_here[kind]))), spread, True)
                parts.append(dot3(green, half) + passed + cross + cross.T)
            full_here = parts
            if i > 0:
                green_here = split(green[0].astype(jnp.float32) + green[1].astype(jnp.float32) + extra)

            @pl.when(slab_index == i)
            def _():
                for kind in range(2):
                    out_ref[kind] = full_here[kind]


def per_device(onsite, hopping, sigma_less, sigma_great, phonon_shift, occupation):
    orbitals = sigma_less.shape[2]
    n_energy = lax.axis_size("energy")
    n_slab = lax.axis_size("slab")
    own = [onsite[0], hopping[0], sigma_less[0, 0], sigma_great[0, 0]]
    operands = list(own)
    for distance in range(1, n_slab):
        route = [((i + distance) % n_slab, i) for i in range(n_slab)]
        operands += [lax.ppermute(block, "slab", route) for block in own]
    payload = pl.pallas_call(
        functools.partial(recursion_kernel, n_slab, n_energy),
        out_shape=jax.ShapeDtypeStruct((2, orbitals, orbitals), jnp.float32),
        in_specs=[pl.BlockSpec(memory_space=pltpu.VMEM)] * len(operands),
        out_specs=pl.BlockSpec(memory_space=pltpu.VMEM),
        scratch_shapes=[
            pltpu.VMEM((orbitals, orbitals), jnp.float32),
            pltpu.VMEM((4, n_slab, orbitals, orbitals), jnp.float32),
        ],
        compiler_params=pltpu.CompilerParams(vmem_limit_bytes=40 * 2**20),
    )(*operands)
    occupancy = occupation[0]
    largest = min(2**OFFSET_BITS, n_energy // 2) - 1

    def moved_by(offset, blocks):
        up = [(i, i + offset) for i in range(n_energy - offset)]
        down = [(i + offset, i) for i in range(n_energy - offset)]
        return (lax.ppermute(blocks, "energy", down), lax.ppermute(blocks, "energy", up))

    above, below = lax.switch(
        phonon_shift[0] - 1,
        [functools.partial(moved_by, offset) for offset in range(1, largest + 1)],
        payload,
    )
    next_less = (occupancy + 1.0) * above[0] + occupancy * below[0]
    next_great = (occupancy + 1.0) * below[1] + occupancy * above[1]
    return (next_less[None, None], next_great[None, None])


def solution(mesh):
    in_specs = (
        P("slab", None, None),
        P("slab", None, None),
        P("energy", "slab", None, None),
        P("energy", "slab", None, None),
        P(),
        P(),
    )
    out_specs = (P("energy", "slab", None, None), P("energy", "slab", None, None))
    return jax.shard_map(
        per_device, mesh=mesh, in_specs=in_specs, out_specs=out_specs, check_vma=False
    )
```

```python
import functools
import jax
import jax.numpy as jnp
from jax import lax
from jax.experimental import pallas as pl
from jax.experimental.pallas import tpu as pltpu
from jax.sharding import PartitionSpec as P

OFFSET_BITS = 4


def split(matrix):
    high = matrix.astype(jnp.bfloat16)
    return high, (matrix - high.astype(jnp.float32)).astype(jnp.bfloat16)


def dot_pass(first, second, transposed):
    contract = (((1,), (1 if transposed else 0,)), ((), ()))
    return lax.dot_general(first, second, contract, preferred_element_type=jnp.float32)


def dot3(first, second, transposed=False):
    small = dot_pass(first[0], second[1], transposed) + dot_pass(first[1], second[0], transposed)
    return dot_pass(first[0], second[0], transposed) + small


def unit_matrix(orbitals):
    rows = lax.broadcasted_iota(jnp.int32, (orbitals, orbitals), 0)
    columns = lax.broadcasted_iota(jnp.int32, (orbitals, orbitals), 1)
    return rows == columns


def invert_definite(matrix, x_ref):
    orbitals = matrix.shape[0]
    on_diagonal = unit_matrix(orbitals)
    matrix = 0.5 * (matrix + matrix.T)
    diagonal = jnp.where(on_diagonal, matrix, 0.0)
    scale = lax.rsqrt(jnp.sum(diagonal, 0, keepdims=True)) * lax.rsqrt(jnp.sum(diagonal, 1, keepdims=True))
    scaled = matrix * scale
    reach = jnp.max(jnp.sum(jnp.abs(scaled), 1, keepdims=True))
    weight = jnp.minimum(1.0, 1.96 / reach)
    x_ref[...] = jnp.where(on_diagonal, 2.0 * weight, 0.0) - (weight * weight) * scaled
    scaled_parts = split(scaled)

    def going_on(state):
        step, residual = state
        return jnp.logical_and(step < 60, residual > 4e-6)

    def refine(state):
        step, _ = state
        x_parts = split(x_ref[...])
        gap = jnp.where(on_diagonal, 1.0, 0.0) - dot3(scaled_parts, x_parts)
        x_ref[...] += dot3(x_parts, split(gap))
        return step + 1, jnp.sum(gap * gap)

    lax.while_loop(going_on, refine, (jnp.int32(0), jnp.float32(1.0)))
    return x_ref[...] * scale


def gather_kernel(n_slab, *refs):
    own, (gathered, own_done, sent, arrived) = refs[:4], refs[4:]
    me = lax.axis_index("slab")
    energy = lax.axis_index("energy")
    others = [lax.rem(me + distance, n_slab) for distance in range(1, n_slab)]
    local = [
        pltpu.make_async_copy(own[kind], gathered.at[kind, me], own_done.at[kind]) for kind in range(4)
    ]
    barrier = pltpu.get_barrier_semaphore()
    for other in others:
        pl.semaphore_signal(barrier, inc=1, device_id=(energy, other), device_id_type=pl.DeviceIdType.MESH)
    for copy in local:
        copy.start()
    pl.semaphore_wait(barrier, n_slab - 1)
    copies = [
        pltpu.make_async_remote_copy(
            src_ref=own[kind],
            dst_ref=gathered.at[kind, me],
            send_sem=sent.at[kind, distance],
            recv_sem=arrived.at[kind, distance],
            device_id=(energy, other),
            device_id_type=pl.DeviceIdType.MESH,
        )
        for distance, other in enumerate(others)
        for kind in range(4)
    ]
    for copy in copies:
        copy.start()
    for copy in local + copies:
        copy.wait()


def recursion_kernel(n_slab, n_energy, arrays, out_ref, x_ref):
    slab_index = lax.axis_index("slab")
    energy = lax.axis_index("energy").astype(jnp.float32)
    orbitals = x_ref.shape[0]
    shift = jnp.where(unit_matrix(orbitals), 0.05 + 0.2 * energy / n_energy, 0.0)
    greens, inners, spreads = [], [], []
    for i in range(n_slab):
        coupling = arrays[1, i]
        coupling_t = split(coupling.T)
        sources = [arrays[2, i], arrays[3, i]]
        block = arrays[0, i] + shift + 0.5 * (sources[0] + sources[1])
        if i == 0:
            coupled = dot3(coupling_t, split(coupling))
        else:
            spread = dot3(greens[-1], split(coupling))
            spread_parts = split(spread)
            coupled = dot3(coupling_t, spread_parts)
            spread_t = split(spread.T)
            sources = [
                source + dot3(spread_t, split(dot3(split(inner), spread_parts)))
                for source, inner in zip(sources, inners[-1])
            ]
            spreads.append(spread_parts)
        greens.append(split(invert_definite(block - coupled, x_ref)))
        inners.append(sources)

    green_full = greens[-1]
    full = [dot3(split(dot3(greens[-1], split(inner))), greens[-1]) for inner in inners[-1]]

    @pl.when(slab_index == n_slab - 1)
    def _():
        for kind in range(2):
            out_ref[kind] = full[kind]

    @pl.when(slab_index < n_slab - 1)
    def _():
        full_here, green_here = full, green_full
        for i in reversed(range(n_slab - 1)):
            green, spread = greens[i], spreads[i]
            extra = dot3(split(dot3(spread, green_here)), spread, True)
            extra_parts = split(extra)
            parts = []
            for kind in range(2):
                half = split(dot3(split(inners[i][kind]), green))
                cross = dot3(extra_parts, half)
                passed = dot3(split(dot3(spread, split(full_here[kind]))), spread, True)
                parts.append(dot3(green, half) + passed + cross + cross.T)
            full_here = parts
            if i > 0:
                green_here = split(green[0].astype(jnp.float32) + green[1].astype(jnp.float32) + extra)

            @pl.when(slab_index == i)
            def _():
                for kind in range(2):
                    out_ref[kind] = full_here[kind]


CHUNKS = 8
MESH = pl.DeviceIdType.MESH


def shift_kernel(offset, relayed, n_energy, occupation_ref, payload, less_ref, great_ref, held, above, below, *semaphores):
    hand_send, hand_recv, up_send, up_recv, down_send, down_recv = semaphores
    me = lax.axis_index("energy")
    slab = lax.axis_index("slab")
    digit = offset & -offset
    direct_end = relayed and digit == offset
    orbitals = payload.shape[1]
    rows = 2 * orbitals // CHUNKS

    def partner_of(place):
        return place + digit * (1 - 2 * ((place // digit) % 2)) if relayed else place

    partner = partner_of(me)
    has_above, has_below = me + offset < n_energy, me - offset >= 0
    to_up, to_down = partner + offset < n_energy, partner - offset >= 0
    from_up, from_down = has_above, has_below
    partner_is_above = partner == me + offset
    if direct_end:
        to_up = jnp.logical_and(to_up, partner + offset != me)
        to_down = jnp.logical_and(to_down, partner - offset != me)
        from_up = jnp.logical_and(from_up, partner != me + offset)
        from_down = jnp.logical_and(from_down, partner != me - offset)

    barrier = pltpu.get_barrier_semaphore()

    def greet(place):
        pl.semaphore_signal(barrier, inc=1, device_id=(place, slab), device_id_type=MESH)

    if relayed:
        greet(partner)
    pl.when(from_up)(lambda: greet(partner_of(me + offset)))
    pl.when(from_down)(lambda: greet(partner_of(me - offset)))
    pl.semaphore_wait(barrier, int(relayed) + to_up.astype(jnp.int32) + to_down.astype(jnp.int32))

    def piece(ref, chunk):
        per_kind = CHUNKS // 2
        return ref.at[chunk // per_kind, pl.ds((chunk % per_kind) * rows, rows)]

    def copy(source, target, chunk, send, recv, place):
        return pltpu.make_async_remote_copy(
            src_ref=piece(source, chunk),
            dst_ref=piece(target, chunk),
            send_sem=send.at[chunk],
            recv_sem=recv.at[chunk],
            device_id=(place, slab),
            device_id_type=MESH,
        )

    order = [kind * (CHUNKS // 2) + part for part in range(CHUNKS // 2) for kind in range(2)]
    passing = held if relayed else payload

    def hand(chunk):
        return copy(payload, held, chunk, hand_send, hand_recv, partner)

    def up(chunk):
        return copy(passing, below, chunk, up_send, up_recv, partner + offset)

    def down(chunk):
        return copy(passing, above, chunk, down_send, down_recv, partner - offset)

    if relayed:
        for chunk in order:
            hand(chunk).start()

    @pl.when(jnp.logical_not(has_above))
    def _():
        above[...] = jnp.zeros_like(above)

    @pl.when(jnp.logical_not(has_below))
    def _():
        below[...] = jnp.zeros_like(below)

    for chunk in order:
        if relayed:
            hand(chunk).wait_recv()
        pl.when(to_up)(lambda: up(chunk).start())
        pl.when(to_down)(lambda: down(chunk).start())

    occupancy = occupation_ref[0]

    def combine(chunk, above_ref, below_ref):
        here_above, here_below = piece(above_ref, chunk)[...], piece(below_ref, chunk)[...]
        place = pl.ds((chunk % (CHUNKS // 2)) * rows, rows)
        if chunk < CHUNKS // 2:
            less_ref[place] = (occupancy + 1.0) * here_above + occupancy * here_below
        else:
            great_ref[place] = (occupancy + 1.0) * here_below + occupancy * here_above

    for chunk in order:
        pl.when(from_up)(lambda: down(chunk).wait_recv())
        pl.when(from_down)(lambda: up(chunk).wait_recv())
        if direct_end:
            pl.when(partner_is_above)(lambda: combine(chunk, held, below))
            pl.when(jnp.logical_not(partner_is_above))(lambda: combine(chunk, above, held))
        else:
            combine(chunk, above, below)
    for chunk in order:
        if relayed:
            hand(chunk).wait_send()
        pl.when(to_up)(lambda: up(chunk).wait_send())
        pl.when(to_down)(lambda: down(chunk).wait_send())


def shifted_sum(offset, occupation, payload):
    n_energy = lax.axis_size("energy")
    orbitals = payload.shape[1]
    relayed = offset % 4 != 0
    blocks = pltpu.VMEM((2, orbitals, orbitals), jnp.float32)
    return pl.pallas_call(
        functools.partial(shift_kernel, offset, relayed, n_energy),
        out_shape=[jax.ShapeDtypeStruct((orbitals, orbitals), jnp.float32)] * 2,
        in_specs=[pl.BlockSpec(memory_space=pltpu.SMEM), pl.BlockSpec(memory_space=pltpu.VMEM)],
        out_specs=[pl.BlockSpec(memory_space=pltpu.VMEM)] * 2,
        scratch_shapes=[blocks] * 3 + [pltpu.SemaphoreType.DMA((CHUNKS,))] * 6,
        compiler_params=pltpu.CompilerParams(
            collective_id=offset, has_side_effects=True, vmem_limit_bytes=16 * 2**20
        ),
    )(occupation, payload)


def per_device(onsite, hopping, sigma_less, sigma_great, phonon_shift, occupation):
    orbitals = sigma_less.shape[2]
    n_energy = lax.axis_size("energy")
    n_slab = lax.axis_size("slab")
    own = [onsite[0], hopping[0], sigma_less[0, 0], sigma_great[0, 0]]
    gathered = pl.pallas_call(
        functools.partial(gather_kernel, n_slab),
        out_shape=jax.ShapeDtypeStruct((4, n_slab, orbitals, orbitals), jnp.float32),
        in_specs=[pl.BlockSpec(memory_space=pl.ANY)] * 4,
        out_specs=pl.BlockSpec(memory_space=pltpu.VMEM),
        scratch_shapes=[pltpu.SemaphoreType.DMA((4,))] + [pltpu.SemaphoreType.DMA((4, n_slab))] * 2,
        compiler_params=pltpu.CompilerParams(
            collective_id=0, has_side_effects=True, vmem_limit_bytes=60 * 2**20
        ),
    )(*own)
    payload = pl.pallas_call(
        functools.partial(recursion_kernel, n_slab, n_energy),
        out_shape=jax.ShapeDtypeStruct((2, orbitals, orbitals), jnp.float32),
        in_specs=[pl.BlockSpec(memory_space=pltpu.VMEM)],
        out_specs=pl.BlockSpec(memory_space=pltpu.VMEM),
        scratch_shapes=[
            pltpu.VMEM((orbitals, orbitals), jnp.float32),
        ],
        compiler_params=pltpu.CompilerParams(vmem_limit_bytes=40 * 2**20),
    )(gathered)
    largest = min(2**OFFSET_BITS, n_energy // 2) - 1

    next_less, next_great = lax.switch(
        phonon_shift[0] - 1,
        [functools.partial(shifted_sum, offset) for offset in range(1, largest + 1)],
        occupation,
        payload,
    )
    return (next_less[None, None], next_great[None, None])


def solution(mesh):
    in_specs = (
        P("slab", None, None),
        P("slab", None, None),
        P("energy", "slab", None, None),
        P("energy", "slab", None, None),
        P(),
        P(),
    )
    out_specs = (P("energy", "slab", None, None), P("energy", "slab", None, None))
    return jax.shard_map(
        per_device, mesh=mesh, in_specs=in_specs, out_specs=out_specs, check_vma=False
    )
```

```python
import functools
import jax
import jax.numpy as jnp
from jax import lax
from jax.experimental import pallas as pl
from jax.experimental.pallas import tpu as pltpu
from jax.sharding import PartitionSpec as P

OFFSET_BITS = 4
GATHER_VMEM = 16 * 2**20


def split(matrix):
    high = matrix.astype(jnp.bfloat16)
    return high, (matrix - high.astype(jnp.float32)).astype(jnp.bfloat16)


def dot_pass(first, second, transposed):
    contract = (((1,), (1 if transposed else 0,)), ((), ()))
    return lax.dot_general(first, second, contract, preferred_element_type=jnp.float32)


def dot3(first, second, transposed=False):
    small = dot_pass(first[0], second[1], transposed) + dot_pass(first[1], second[0], transposed)
    return dot_pass(first[0], second[0], transposed) + small


def unit_matrix(orbitals):
    rows = lax.broadcasted_iota(jnp.int32, (orbitals, orbitals), 0)
    columns = lax.broadcasted_iota(jnp.int32, (orbitals, orbitals), 1)
    return rows == columns


def invert_definite(matrix, x_ref):
    orbitals = matrix.shape[0]
    on_diagonal = unit_matrix(orbitals)
    matrix = 0.5 * (matrix + matrix.T)
    diagonal = jnp.where(on_diagonal, matrix, 0.0)
    scale = lax.rsqrt(jnp.sum(diagonal, 0, keepdims=True)) * lax.rsqrt(jnp.sum(diagonal, 1, keepdims=True))
    scaled = matrix * scale
    reach = jnp.max(jnp.sum(jnp.abs(scaled), 1, keepdims=True))
    weight = jnp.minimum(1.0, 1.96 / reach)
    x_ref[...] = jnp.where(on_diagonal, 2.0 * weight, 0.0) - (weight * weight) * scaled
    scaled_parts = split(scaled)

    def going_on(state):
        step, residual = state
        return jnp.logical_and(step < 60, residual > 4e-6)

    def refine(state):
        step, _ = state
        x_parts = split(x_ref[...])
        gap = jnp.where(on_diagonal, 1.0, 0.0) - dot3(scaled_parts, x_parts)
        x_ref[...] += dot3(x_parts, split(gap))
        return step + 1, jnp.sum(gap * gap)

    lax.while_loop(going_on, refine, (jnp.int32(0), jnp.float32(1.0)))
    return x_ref[...] * scale


def gather_kernel(n_slab, kinds, *refs):
    own, (gathered, own_done, sent, arrived) = refs[:-4], refs[-4:]
    me = lax.axis_index("slab")
    energy = lax.axis_index("energy")
    others = [lax.rem(me + distance, n_slab) for distance in range(1, n_slab)]
    if len(own) == 1:
        own = [own[0].at[kind] for kind in range(kinds)]
    local = [
        pltpu.make_async_copy(own[kind], gathered.at[kind, me], own_done.at[kind]) for kind in range(kinds)
    ]
    barrier = pltpu.get_barrier_semaphore()
    for other in others:
        pl.semaphore_signal(barrier, inc=1, device_id=(energy, other), device_id_type=pl.DeviceIdType.MESH)
    for copy in local:
        copy.start()
    pl.semaphore_wait(barrier, n_slab - 1)
    copies = [
        pltpu.make_async_remote_copy(
            src_ref=own[kind],
            dst_ref=gathered.at[kind, me],
            send_sem=sent.at[kind, distance],
            recv_sem=arrived.at[kind, distance],
            device_id=(energy, other),
            device_id_type=pl.DeviceIdType.MESH,
        )
        for distance, other in enumerate(others)
        for kind in range(kinds)
    ]
    for copy in copies:
        copy.start()
    for copy in local + copies:
        copy.wait()


def gather_slabs(own, kinds, call_number):
    n_slab = lax.axis_size("slab")
    orbitals = own[0].shape[-1]
    return pl.pallas_call(
        functools.partial(gather_kernel, n_slab, kinds),
        out_shape=jax.ShapeDtypeStruct((kinds, n_slab, orbitals, orbitals), jnp.float32),
        in_specs=[pl.BlockSpec(memory_space=pl.ANY)] * len(own),
        out_specs=pl.BlockSpec(memory_space=pl.ANY),
        scratch_shapes=[pltpu.SemaphoreType.DMA((kinds,))] + [pltpu.SemaphoreType.DMA((kinds, n_slab))] * 2,
        compiler_params=pltpu.CompilerParams(
            collective_id=call_number, has_side_effects=True, vmem_limit_bytes=GATHER_VMEM
        ),
    )(*own)


def recursion_body(n_slab, n_energy, energy, first_sigma, arrays, sigma, out_ref, x_ref):
    slab_index = lax.axis_index("slab")
    energy = energy.astype(jnp.float32)
    orbitals = x_ref.shape[0]
    shift = jnp.where(unit_matrix(orbitals), 0.05 + 0.2 * energy / n_energy, 0.0)
    greens, inners, spreads = [], [], []
    for i in range(n_slab):
        coupling = arrays[1, i]
        coupling_t = split(coupling.T)
        sources = [sigma[first_sigma, i], sigma[first_sigma + 1, i]]
        block = arrays[0, i] + shift + 0.5 * (sources[0] + sources[1])
        if i == 0:
            coupled = dot3(coupling_t, split(coupling))
        else:
            spread = dot3(greens[-1], split(coupling))
            spread_parts = split(spread)
            coupled = dot3(coupling_t, spread_parts)
            spread_t = split(spread.T)
            sources = [
                source + dot3(spread_t, split(dot3(split(inner), spread_parts)))
                for source, inner in zip(sources, inners[-1])
            ]
            spreads.append(spread_parts)
        greens.append(split(invert_definite(block - coupled, x_ref)))
        inners.append(sources)

    green_full = greens[-1]
    full = [dot3(split(dot3(greens[-1], split(inner))), greens[-1]) for inner in inners[-1]]

    @pl.when(slab_index == n_slab - 1)
    def _():
        for kind in range(2):
            out_ref[kind] = full[kind]

    @pl.when(slab_index < n_slab - 1)
    def _():
        full_here, green_here = full, green_full
        for i in reversed(range(n_slab - 1)):
            green, spread = greens[i], spreads[i]
            extra = dot3(split(dot3(spread, green_here)), spread, True)
            extra_parts = split(extra)
            parts = []
            for kind in range(2):
                half = split(dot3(split(inners[i][kind]), green))
                cross = dot3(extra_parts, half)
                passed = dot3(split(dot3(spread, split(full_here[kind]))), spread, True)
                parts.append(dot3(green, half) + passed + cross + cross.T)
            full_here = parts
            if i > 0:
                green_here = split(green[0].astype(jnp.float32) + green[1].astype(jnp.float32) + extra)

            @pl.when(slab_index == i)
            def _():
                for kind in range(2):
                    out_ref[kind] = full_here[kind]


def taken_from(place, offset):
    return ((place + offset) % (2 * offset)) // 4 % 2 == 0


def recursion_kernel(n_slab, n_energy, offset, *refs):
    me = lax.axis_index("energy")
    if offset == 0:
        arrays, out_ref, x_ref = refs
        recursion_body(n_slab, n_energy, me, 2, arrays, arrays, out_ref, x_ref)
        return
    arrays, sigma, out_ref, x_ref = refs
    energy = jnp.where(taken_from(me, offset), me - offset, me + offset)
    inside = jnp.logical_and(energy >= 0, energy < n_energy)

    @pl.when(inside)
    def _():
        recursion_body(n_slab, n_energy, energy, 0, arrays, sigma, out_ref, x_ref)

    @pl.when(jnp.logical_not(inside))
    def _():
        out_ref[...] = jnp.zeros_like(out_ref)


def full_blocks(offset, *gathered):
    n_energy = lax.axis_size("energy")
    n_slab = lax.axis_size("slab")
    orbitals = gathered[0].shape[-1]
    return pl.pallas_call(
        functools.partial(recursion_kernel, n_slab, n_energy, offset),
        out_shape=jax.ShapeDtypeStruct((2, orbitals, orbitals), jnp.float32),
        in_specs=[pl.BlockSpec(memory_space=pltpu.VMEM)] * len(gathered),
        out_specs=pl.BlockSpec(memory_space=pltpu.VMEM),
        scratch_shapes=[pltpu.VMEM((orbitals, orbitals), jnp.float32)],
        compiler_params=pltpu.CompilerParams(vmem_limit_bytes=32 * 2**20),
        cost_estimate=pl.CostEstimate(flops=10**10, bytes_accessed=2**20, transcendentals=0),
    )(*gathered)


def shifted_sum(offset, own, occupation):
    n_energy = lax.axis_size("energy")
    me = lax.axis_index("energy")
    early, late = [], []
    for place in range(n_energy):
        lower, higher = (place - offset, place), (place + offset, place)
        first, second = (lower, higher) if taken_from(place, offset) else (higher, lower)
        early += [first] if 0 <= first[0] < n_energy else []
        late += [second] if 0 <= second[0] < n_energy else []
    sigma = lax.ppermute(jnp.stack(own[2:]), "energy", early)
    gathered = gather_slabs(own, 4, offset)
    payload = full_blocks(0, gathered)
    received = lax.ppermute(payload, "energy", late)
    sigma = lax.optimization_barrier((sigma, payload))[0]
    computed = full_blocks(offset, gathered, gather_slabs([sigma], 2, 2**OFFSET_BITS + offset))
    from_lower = taken_from(me, offset).astype(jnp.float32)
    computed_less = occupation[0] + (1.0 - from_lower)
    computed_great = occupation[0] + from_lower
    next_less = computed_less * computed[0] + computed_great * received[0]
    next_great = computed_great * computed[1] + computed_less * received[1]
    return next_less, next_great


def per_device(onsite, hopping, sigma_less, sigma_great, phonon_shift, occupation):
    largest = min(2**OFFSET_BITS, lax.axis_size("energy") // 2) - 1
    own = [onsite[0], hopping[0], sigma_less[0, 0], sigma_great[0, 0]]
    next_less, next_great = lax.switch(
        phonon_shift[0] - 1,
        [functools.partial(shifted_sum, offset) for offset in range(1, largest + 1)],
        own,
        occupation,
    )
    return (next_less[None, None], next_great[None, None])


def solution(mesh):
    in_specs = (
        P("slab", None, None),
        P("slab", None, None),
        P("energy", "slab", None, None),
        P("energy", "slab", None, None),
        P(),
        P(),
    )
    out_specs = (P("energy", "slab", None, None), P("energy", "slab", None, None))
    return jax.shard_map(
        per_device, mesh=mesh, in_specs=in_specs, out_specs=out_specs, check_vma=False
    )
```

```python
import functools
import jax
import jax.numpy as jnp
from jax import lax
from jax.experimental import pallas as pl
from jax.experimental.pallas import tpu as pltpu
from jax.sharding import PartitionSpec as P

OFFSET_BITS = 4


def split(matrix):
    high = matrix.astype(jnp.bfloat16)
    return high, (matrix - high.astype(jnp.float32)).astype(jnp.bfloat16)


def dot_pass(first, second, transposed):
    contract = (((1,), (1 if transposed else 0,)), ((), ()))
    return lax.dot_general(first, second, contract, preferred_element_type=jnp.float32)


def dot3(first, second, transposed=False):
    small = dot_pass(first[0], second[1], transposed) + dot_pass(first[1], second[0], transposed)
    return dot_pass(first[0], second[0], transposed) + small


def unit_matrix(orbitals):
    rows = lax.broadcasted_iota(jnp.int32, (orbitals, orbitals), 0)
    columns = lax.broadcasted_iota(jnp.int32, (orbitals, orbitals), 1)
    return rows == columns


def invert_definite(matrix, x_ref):
    orbitals = matrix.shape[0]
    on_diagonal = unit_matrix(orbitals)
    matrix = 0.5 * (matrix + matrix.T)
    diagonal = jnp.where(on_diagonal, matrix, 0.0)
    scale = lax.rsqrt(jnp.sum(diagonal, 0, keepdims=True)) * lax.rsqrt(jnp.sum(diagonal, 1, keepdims=True))
    scaled = matrix * scale
    reach = jnp.max(jnp.sum(jnp.abs(scaled), 1, keepdims=True))
    weight = jnp.minimum(1.0, 1.96 / reach)
    x_ref[...] = jnp.where(on_diagonal, 2.0 * weight, 0.0) - (weight * weight) * scaled
    scaled_parts = split(scaled)

    def going_on(state):
        step, residual = state
        return jnp.logical_and(step < 60, residual > 4e-6)

    def refine(state):
        step, _ = state
        x_parts = split(x_ref[...])
        gap = jnp.where(on_diagonal, 1.0, 0.0) - dot3(scaled_parts, x_parts)
        x_ref[...] += dot3(x_parts, split(gap))
        return step + 1, jnp.sum(gap * gap)

    lax.while_loop(going_on, refine, (jnp.int32(0), jnp.float32(1.0)))
    return x_ref[...] * scale


def gather_kernel(n_slab, *refs):
    own, (gathered, own_done, sent, arrived) = refs[:4], refs[4:]
    me = lax.axis_index("slab")
    energy = lax.axis_index("energy")
    others = [lax.rem(me + distance, n_slab) for distance in range(1, n_slab)]
    local = [
        pltpu.make_async_copy(own[kind], gathered.at[kind, me], own_done.at[kind]) for kind in range(4)
    ]
    barrier = pltpu.get_barrier_semaphore()
    for other in others:
        pl.semaphore_signal(barrier, inc=1, device_id=(energy, other), device_id_type=pl.DeviceIdType.MESH)
    for copy in local:
        copy.start()
    pl.semaphore_wait(barrier, n_slab - 1)
    copies = [
        pltpu.make_async_remote_copy(
            src_ref=own[kind],
            dst_ref=gathered.at[kind, me],
            send_sem=sent.at[kind, distance],
            recv_sem=arrived.at[kind, distance],
            device_id=(energy, other),
            device_id_type=pl.DeviceIdType.MESH,
        )
        for distance, other in enumerate(others)
        for kind in range(4)
    ]
    for copy in copies:
        copy.start()
    for copy in local + copies:
        copy.wait()


def recursion_kernel(n_slab, n_energy, gathered, out_ref, x_ref, arrays, arrived):
    loads = {
        (kind, i): pltpu.make_async_copy(gathered.at[kind, i], arrays.at[kind, i], arrived.at[kind, i])
        for i in range(n_slab)
        for kind in (1, 2, 3, 0)
    }
    for load in loads.values():
        load.start()

    def loaded(kind, i):
        loads[kind, i].wait()
        return arrays[kind, i]

    slab_index = lax.axis_index("slab")
    energy = lax.axis_index("energy").astype(jnp.float32)
    orbitals = x_ref.shape[0]
    shift = jnp.where(unit_matrix(orbitals), 0.05 + 0.2 * energy / n_energy, 0.0)
    greens, inners, spreads = [], [], []
    for i in range(n_slab):
        coupling = loaded(1, i)
        coupling_t = split(coupling.T)
        sources = [loaded(2, i), loaded(3, i)]
        block = loaded(0, i) + shift + 0.5 * (sources[0] + sources[1])
        if i == 0:
            coupled = dot3(coupling_t, split(coupling))
        else:
            spread = dot3(greens[-1], split(coupling))
            spread_parts = split(spread)
            coupled = dot3(coupling_t, spread_parts)
            spread_t = split(spread.T)
            sources = [
                source + dot3(spread_t, split(dot3(split(inner), spread_parts)))
                for source, inner in zip(sources, inners[-1])
            ]
            spreads.append(spread_parts)
        greens.append(split(invert_definite(block - coupled, x_ref)))
        inners.append(sources)

    green_full = greens[-1]
    full = [dot3(split(dot3(greens[-1], split(inner))), greens[-1]) for inner in inners[-1]]

    @pl.when(slab_index == n_slab - 1)
    def _():
        for kind in range(2):
            out_ref[kind] = full[kind]

    @pl.when(slab_index < n_slab - 1)
    def _():
        full_here, green_here = full, green_full
        for i in reversed(range(n_slab - 1)):
            green, spread = greens[i], spreads[i]
            extra = dot3(split(dot3(spread, green_here)), spread, True)
            extra_parts = split(extra)
            parts = []
            for kind in range(2):
                half = split(dot3(split(inners[i][kind]), green))
                cross = dot3(extra_parts, half)
                passed = dot3(split(dot3(spread, split(full_here[kind]))), spread, True)
                parts.append(dot3(green, half) + passed + cross + cross.T)
            full_here = parts
            if i > 0:
                green_here = split(green[0].astype(jnp.float32) + green[1].astype(jnp.float32) + extra)

            @pl.when(slab_index == i)
            def _():
                for kind in range(2):
                    out_ref[kind] = full_here[kind]


CHUNKS = 8
MESH = pl.DeviceIdType.MESH


def shift_kernel(offset, relay_count, n_energy, occupation_ref, payload, less_ref, great_ref, held, above, below, *semaphores):
    hand_send, hand_recv, up_send, up_recv, down_send, down_recv = semaphores
    me = lax.axis_index("energy")
    slab = lax.axis_index("slab")
    digit = offset & -offset
    relayed = relay_count > 0
    straight = relay_count < CHUNKS
    direct_end = relayed and digit == offset
    orbitals = payload.shape[1]
    rows = 2 * orbitals // CHUNKS

    def partner_of(place):
        return place + digit * (1 - 2 * ((place // digit) % 2)) if relayed else place

    partner = partner_of(me)
    has_above, has_below = me + offset < n_energy, me - offset >= 0
    to_up, to_down = partner + offset < n_energy, partner - offset >= 0
    from_up, from_down = has_above, has_below
    partner_is_above = partner == me + offset
    if direct_end:
        to_up = jnp.logical_and(to_up, partner + offset != me)
        to_down = jnp.logical_and(to_down, partner - offset != me)
        from_up = jnp.logical_and(from_up, partner != me + offset)
        from_down = jnp.logical_and(from_down, partner != me - offset)

    barrier = pltpu.get_barrier_semaphore()

    def greet(place):
        pl.semaphore_signal(barrier, inc=1, device_id=(place, slab), device_id_type=MESH)

    if relayed:
        greet(partner)
        pl.when(from_up)(lambda: greet(partner_of(me + offset)))
        pl.when(from_down)(lambda: greet(partner_of(me - offset)))
    if straight:
        pl.when(has_above)(lambda: greet(me + offset))
        pl.when(has_below)(lambda: greet(me - offset))
    expected = 0
    if relayed:
        expected += 1 + to_up.astype(jnp.int32) + to_down.astype(jnp.int32)
    if straight:
        expected += has_above.astype(jnp.int32) + has_below.astype(jnp.int32)
    pl.semaphore_wait(barrier, expected)

    def piece(ref, chunk):
        per_kind = CHUNKS // 2
        return ref.at[chunk // per_kind, pl.ds((chunk % per_kind) * rows, rows)]

    def copy(source, target, chunk, send, recv, place):
        return pltpu.make_async_remote_copy(
            src_ref=piece(source, chunk),
            dst_ref=piece(target, chunk),
            send_sem=send.at[chunk],
            recv_sem=recv.at[chunk],
            device_id=(place, slab),
            device_id_type=MESH,
        )

    order = [kind * (CHUNKS // 2) + part for part in range(CHUNKS // 2) for kind in range(2)]
    by_relay, at_once = order[:relay_count], order[relay_count:]

    def hand(chunk):
        return copy(payload, held, chunk, hand_send, hand_recv, partner)

    def up(chunk):
        if chunk in by_relay:
            return copy(held, below, chunk, up_send, up_recv, partner + offset)
        return copy(payload, below, chunk, up_send, up_recv, me + offset)

    def down(chunk):
        if chunk in by_relay:
            return copy(held, above, chunk, down_send, down_recv, partner - offset)
        return copy(payload, above, chunk, down_send, down_recv, me - offset)

    def goes_up(chunk):
        return to_up if chunk in by_relay else has_above

    def goes_down(chunk):
        return to_down if chunk in by_relay else has_below

    for chunk in by_relay:
        hand(chunk).start()
    for chunk in at_once:
        pl.when(has_above)(lambda: up(chunk).start())
        pl.when(has_below)(lambda: down(chunk).start())

    @pl.when(jnp.logical_not(has_above))
    def _():
        above[...] = jnp.zeros_like(above)

    @pl.when(jnp.logical_not(has_below))
    def _():
        below[...] = jnp.zeros_like(below)

    for chunk in by_relay:
        hand(chunk).wait_recv()
        pl.when(to_up)(lambda: up(chunk).start())
        pl.when(to_down)(lambda: down(chunk).start())

    occupancy = occupation_ref[0]

    def combine(chunk, above_ref, below_ref):
        here_above, here_below = piece(above_ref, chunk)[...], piece(below_ref, chunk)[...]
        place = pl.ds((chunk % (CHUNKS // 2)) * rows, rows)
        if chunk < CHUNKS // 2:
            less_ref[place] = (occupancy + 1.0) * here_above + occupancy * here_below
        else:
            great_ref[place] = (occupancy + 1.0) * here_below + occupancy * here_above

    for chunk in order:
        pl.when(from_up)(lambda: down(chunk).wait_recv())
        pl.when(from_down)(lambda: up(chunk).wait_recv())
        if direct_end:
            pl.when(partner_is_above)(lambda: combine(chunk, held, below))
            pl.when(jnp.logical_not(partner_is_above))(lambda: combine(chunk, above, held))
        else:
            combine(chunk, above, below)
    for chunk in order:
        if chunk in by_relay:
            hand(chunk).wait_send()
        pl.when(goes_up(chunk))(lambda: up(chunk).wait_send())
        pl.when(goes_down(chunk))(lambda: down(chunk).wait_send())


def relay_chunks(offset):
    if offset % 4 == 0:
        return 0
    if offset < 4:
        return CHUNKS
    return 0 if offset == 7 else CHUNKS // 2


def shifted_sum(offset, occupation, payload):
    n_energy = lax.axis_size("energy")
    orbitals = payload.shape[1]
    relay_count = relay_chunks(offset)
    blocks = pltpu.VMEM((2, orbitals, orbitals), jnp.float32)
    return pl.pallas_call(
        functools.partial(shift_kernel, offset, relay_count, n_energy),
        out_shape=[jax.ShapeDtypeStruct((orbitals, orbitals), jnp.float32)] * 2,
        in_specs=[pl.BlockSpec(memory_space=pltpu.SMEM), pl.BlockSpec(memory_space=pltpu.VMEM)],
        out_specs=[pl.BlockSpec(memory_space=pltpu.VMEM)] * 2,
        scratch_shapes=[blocks] * 3 + [pltpu.SemaphoreType.DMA((CHUNKS,))] * 6,
        compiler_params=pltpu.CompilerParams(
            collective_id=offset, has_side_effects=True, vmem_limit_bytes=16 * 2**20
        ),
    )(occupation, payload)


def per_device(onsite, hopping, sigma_less, sigma_great, phonon_shift, occupation):
    orbitals = sigma_less.shape[2]
    n_energy = lax.axis_size("energy")
    n_slab = lax.axis_size("slab")
    own = [onsite[0], hopping[0], sigma_less[0, 0], sigma_great[0, 0]]
    gathered = pl.pallas_call(
        functools.partial(gather_kernel, n_slab),
        out_shape=jax.ShapeDtypeStruct((4, n_slab, orbitals, orbitals), jnp.float32),
        in_specs=[pl.BlockSpec(memory_space=pl.ANY)] * 4,
        out_specs=pl.BlockSpec(memory_space=pl.ANY),
        scratch_shapes=[pltpu.SemaphoreType.DMA((4,))] + [pltpu.SemaphoreType.DMA((4, n_slab))] * 2,
        compiler_params=pltpu.CompilerParams(
            collective_id=0, has_side_effects=True, vmem_limit_bytes=60 * 2**20
        ),
    )(*own)
    payload = pl.pallas_call(
        functools.partial(recursion_kernel, n_slab, n_energy),
        out_shape=jax.ShapeDtypeStruct((2, orbitals, orbitals), jnp.float32),
        in_specs=[pl.BlockSpec(memory_space=pl.ANY)],
        out_specs=pl.BlockSpec(memory_space=pltpu.VMEM),
        scratch_shapes=[
            pltpu.VMEM((orbitals, orbitals), jnp.float32),
            pltpu.VMEM((4, n_slab, orbitals, orbitals), jnp.float32),
            pltpu.SemaphoreType.DMA((4, n_slab)),
        ],
        compiler_params=pltpu.CompilerParams(vmem_limit_bytes=60 * 2**20),
    )(gathered)
    largest = min(2**OFFSET_BITS, n_energy // 2) - 1

    next_less, next_great = lax.switch(
        phonon_shift[0] - 1,
        [functools.partial(shifted_sum, offset) for offset in range(1, largest + 1)],
        occupation,
        payload,
    )
    return (next_less[None, None], next_great[None, None])


def solution(mesh):
    in_specs = (
        P("slab", None, None),
        P("slab", None, None),
        P("energy", "slab", None, None),
        P("energy", "slab", None, None),
        P(),
        P(),
    )
    out_specs = (P("energy", "slab", None, None), P("energy", "slab", None, None))
    return jax.shard_map(
        per_device, mesh=mesh, in_specs=in_specs, out_specs=out_specs, check_vma=False
    )
```

```python
import functools
import jax
import jax.numpy as jnp
from jax import lax
from jax.experimental import pallas as pl
from jax.experimental.pallas import tpu as pltpu
from jax.sharding import PartitionSpec as P

OFFSET_BITS = 4


def split(matrix):
    high = matrix.astype(jnp.bfloat16)
    return high, (matrix - high.astype(jnp.float32)).astype(jnp.bfloat16)


def dot_pass(first, second, transposed):
    contract = (((1,), (1 if transposed else 0,)), ((), ()))
    return lax.dot_general(first, second, contract, preferred_element_type=jnp.float32)


def dot3(first, second, transposed=False):
    small = dot_pass(first[0], second[1], transposed) + dot_pass(first[1], second[0], transposed)
    return dot_pass(first[0], second[0], transposed) + small


def unit_matrix(orbitals):
    rows = lax.broadcasted_iota(jnp.int32, (orbitals, orbitals), 0)
    columns = lax.broadcasted_iota(jnp.int32, (orbitals, orbitals), 1)
    return rows == columns


def invert_definite(matrix, x_ref):
    orbitals = matrix.shape[0]
    on_diagonal = unit_matrix(orbitals)
    matrix = 0.5 * (matrix + matrix.T)
    diagonal = jnp.where(on_diagonal, matrix, 0.0)
    scale = lax.rsqrt(jnp.sum(diagonal, 0, keepdims=True)) * lax.rsqrt(jnp.sum(diagonal, 1, keepdims=True))
    scaled = matrix * scale
    reach = jnp.max(jnp.sum(jnp.abs(scaled), 1, keepdims=True))
    weight = jnp.minimum(1.0, 1.96 / reach)
    x_ref[...] = jnp.where(on_diagonal, 2.0 * weight, 0.0) - (weight * weight) * scaled
    scaled_parts = split(scaled)

    def going_on(state):
        step, residual = state
        return jnp.logical_and(step < 60, residual > 4e-6)

    def refine(state):
        step, _ = state
        x_parts = split(x_ref[...])
        gap = jnp.where(on_diagonal, 1.0, 0.0) - dot3(scaled_parts, x_parts)
        x_ref[...] += dot3(x_parts, split(gap))
        return step + 1, jnp.sum(gap * gap)

    lax.while_loop(going_on, refine, (jnp.int32(0), jnp.float32(1.0)))
    return x_ref[...] * scale


def gather_kernel(n_slab, *refs):
    own, (gathered, own_done, sent, arrived) = refs[:4], refs[4:]
    me = lax.axis_index("slab")
    energy = lax.axis_index("energy")
    others = [lax.rem(me + distance, n_slab) for distance in range(1, n_slab)]
    local = [
        pltpu.make_async_copy(own[kind], gathered.at[kind, me], own_done.at[kind]) for kind in range(4)
    ]
    barrier = pltpu.get_barrier_semaphore()
    for other in others:
        pl.semaphore_signal(barrier, inc=1, device_id=(energy, other), device_id_type=pl.DeviceIdType.MESH)
    for copy in local:
        copy.start()
    pl.semaphore_wait(barrier, n_slab - 1)
    copies = [
        pltpu.make_async_remote_copy(
            src_ref=own[kind],
            dst_ref=gathered.at[kind, me],
            send_sem=sent.at[kind, distance],
            recv_sem=arrived.at[kind, distance],
            device_id=(energy, other),
            device_id_type=pl.DeviceIdType.MESH,
        )
        for distance, other in enumerate(others)
        for kind in range(4)
    ]
    for copy in copies:
        copy.start()
    for copy in local + copies:
        copy.wait()


def recursion_kernel(n_slab, n_energy, arrays, out_ref, x_ref):
    slab_index = lax.axis_index("slab")
    energy = lax.axis_index("energy").astype(jnp.float32)
    orbitals = x_ref.shape[0]
    shift = jnp.where(unit_matrix(orbitals), 0.05 + 0.2 * energy / n_energy, 0.0)
    greens, inners, spreads = [], [], []
    for i in range(n_slab):
        coupling = arrays[1, i]
        coupling_t = split(coupling.T)
        sources = [arrays[2, i], arrays[3, i]]
        block = arrays[0, i] + shift + 0.5 * (sources[0] + sources[1])
        if i == 0:
            coupled = dot3(coupling_t, split(coupling))
        else:
            spread = dot3(greens[-1], split(coupling))
            spread_parts = split(spread)
            coupled = dot3(coupling_t, spread_parts)
            spread_t = split(spread.T)
            sources = [
                source + dot3(spread_t, split(dot3(split(inner), spread_parts)))
                for source, inner in zip(sources, inners[-1])
            ]
            spreads.append(spread_parts)
        greens.append(split(invert_definite(block - coupled, x_ref)))
        inners.append(sources)

    green_full = greens[-1]
    full = [dot3(split(dot3(greens[-1], split(inner))), greens[-1]) for inner in inners[-1]]

    @pl.when(slab_index == n_slab - 1)
    def _():
        for kind in range(2):
            out_ref[kind] = full[kind]

    @pl.when(slab_index < n_slab - 1)
    def _():
        full_here, green_here = full, green_full
        for i in reversed(range(n_slab - 1)):
            green, spread = greens[i], spreads[i]
            extra = dot3(split(dot3(spread, green_here)), spread, True)
            extra_parts = split(extra)
            parts = []
            for kind in range(2):
                half = split(dot3(split(inners[i][kind]), green))
                cross = dot3(extra_parts, half)
                passed = dot3(split(dot3(spread, split(full_here[kind]))), spread, True)
                parts.append(dot3(green, half) + passed + cross + cross.T)
            full_here = parts
            if i > 0:
                green_here = split(green[0].astype(jnp.float32) + green[1].astype(jnp.float32) + extra)

            @pl.when(slab_index == i)
            def _():
                for kind in range(2):
                    out_ref[kind] = full_here[kind]


CHUNKS = 8
MESH = pl.DeviceIdType.MESH


def shift_kernel(offset, relay_count, n_energy, occupation_ref, payload, less_ref, great_ref, held, above, below, *semaphores):
    hand_send, hand_recv, up_send, up_recv, down_send, down_recv = semaphores
    me = lax.axis_index("energy")
    slab = lax.axis_index("slab")
    digit = offset & -offset
    relayed = relay_count > 0
    straight = relay_count < CHUNKS
    direct_end = relayed and digit == offset
    orbitals = payload.shape[1]
    rows = 2 * orbitals // CHUNKS

    def partner_of(place):
        return place + digit * (1 - 2 * ((place // digit) % 2)) if relayed else place

    partner = partner_of(me)
    has_above, has_below = me + offset < n_energy, me - offset >= 0
    to_up, to_down = partner + offset < n_energy, partner - offset >= 0
    from_up, from_down = has_above, has_below
    partner_is_above = partner == me + offset
    if direct_end:
        to_up = jnp.logical_and(to_up, partner + offset != me)
        to_down = jnp.logical_and(to_down, partner - offset != me)
        from_up = jnp.logical_and(from_up, partner != me + offset)
        from_down = jnp.logical_and(from_down, partner != me - offset)

    barrier = pltpu.get_barrier_semaphore()

    def greet(place):
        pl.semaphore_signal(barrier, inc=1, device_id=(place, slab), device_id_type=MESH)

    if relayed:
        greet(partner)
        pl.when(from_up)(lambda: greet(partner_of(me + offset)))
        pl.when(from_down)(lambda: greet(partner_of(me - offset)))
    if straight:
        pl.when(has_above)(lambda: greet(me + offset))
        pl.when(has_below)(lambda: greet(me - offset))
    expected = 0
    if relayed:
        expected += 1 + to_up.astype(jnp.int32) + to_down.astype(jnp.int32)
    if straight:
        expected += has_above.astype(jnp.int32) + has_below.astype(jnp.int32)
    pl.semaphore_wait(barrier, expected)

    def piece(ref, chunk):
        per_kind = CHUNKS // 2
        return ref.at[chunk // per_kind, pl.ds((chunk % per_kind) * rows, rows)]

    def copy(source, target, chunk, send, recv, place):
        return pltpu.make_async_remote_copy(
            src_ref=piece(source, chunk),
            dst_ref=piece(target, chunk),
            send_sem=send.at[chunk],
            recv_sem=recv.at[chunk],
            device_id=(place, slab),
            device_id_type=MESH,
        )

    order = [kind * (CHUNKS // 2) + part for part in range(CHUNKS // 2) for kind in range(2)]
    by_relay, at_once = order[:relay_count], order[relay_count:]

    def hand(chunk):
        return copy(payload, held, chunk, hand_send, hand_recv, partner)

    def up(chunk):
        if chunk in by_relay:
            return copy(held, below, chunk, up_send, up_recv, partner + offset)
        return copy(payload, below, chunk, up_send, up_recv, me + offset)

    def down(chunk):
        if chunk in by_relay:
            return copy(held, above, chunk, down_send, down_recv, partner - offset)
        return copy(payload, above, chunk, down_send, down_recv, me - offset)

    def goes_up(chunk):
        return to_up if chunk in by_relay else has_above

    def goes_down(chunk):
        return to_down if chunk in by_relay else has_below

    for chunk in by_relay:
        hand(chunk).start()
    for chunk in at_once:
        pl.when(has_above)(lambda: up(chunk).start())
        pl.when(has_below)(lambda: down(chunk).start())

    @pl.when(jnp.logical_not(has_above))
    def _():
        above[...] = jnp.zeros_like(above)

    @pl.when(jnp.logical_not(has_below))
    def _():
        below[...] = jnp.zeros_like(below)

    for chunk in by_relay:
        hand(chunk).wait_recv()
        pl.when(to_up)(lambda: up(chunk).start())
        pl.when(to_down)(lambda: down(chunk).start())

    occupancy = occupation_ref[0]

    def combine(chunk, above_ref, below_ref):
        here_above, here_below = piece(above_ref, chunk)[...], piece(below_ref, chunk)[...]
        place = pl.ds((chunk % (CHUNKS // 2)) * rows, rows)
        if chunk < CHUNKS // 2:
            less_ref[place] = (occupancy + 1.0) * here_above + occupancy * here_below
        else:
            great_ref[place] = (occupancy + 1.0) * here_below + occupancy * here_above

    for chunk in order:
        pl.when(from_up)(lambda: down(chunk).wait_recv())
        pl.when(from_down)(lambda: up(chunk).wait_recv())
        if direct_end:
            pl.when(partner_is_above)(lambda: combine(chunk, held, below))
            pl.when(jnp.logical_not(partner_is_above))(lambda: combine(chunk, above, held))
        else:
            combine(chunk, above, below)
    for chunk in order:
        if chunk in by_relay:
            hand(chunk).wait_send()
        pl.when(goes_up(chunk))(lambda: up(chunk).wait_send())
        pl.when(goes_down(chunk))(lambda: down(chunk).wait_send())


def relay_chunks(offset):
    if offset % 4 == 0:
        return 0
    if offset < 4:
        return CHUNKS
    return 0 if offset == 7 else CHUNKS // 2


def shifted_sum(offset, occupation, payload):
    n_energy = lax.axis_size("energy")
    orbitals = payload.shape[1]
    relay_count = relay_chunks(offset)
    blocks = pltpu.VMEM((2, orbitals, orbitals), jnp.float32)
    return pl.pallas_call(
        functools.partial(shift_kernel, offset, relay_count, n_energy),
        out_shape=[jax.ShapeDtypeStruct((orbitals, orbitals), jnp.float32)] * 2,
        in_specs=[pl.BlockSpec(memory_space=pltpu.SMEM), pl.BlockSpec(memory_space=pltpu.VMEM)],
        out_specs=[pl.BlockSpec(memory_space=pltpu.VMEM)] * 2,
        scratch_shapes=[blocks] * 3 + [pltpu.SemaphoreType.DMA((CHUNKS,))] * 6,
        compiler_params=pltpu.CompilerParams(
            collective_id=offset, has_side_effects=True, vmem_limit_bytes=16 * 2**20
        ),
    )(occupation, payload)


def per_device(onsite, hopping, sigma_less, sigma_great, phonon_shift, occupation):
    orbitals = sigma_less.shape[2]
    n_energy = lax.axis_size("energy")
    n_slab = lax.axis_size("slab")
    own = [onsite[0], hopping[0], sigma_less[0, 0], sigma_great[0, 0]]
    gather = pl.pallas_call(
        functools.partial(gather_kernel, n_slab),
        out_shape=jax.ShapeDtypeStruct((4, n_slab, orbitals, orbitals), jnp.float32),
        in_specs=[pl.BlockSpec(memory_space=pl.ANY)] * 4,
        out_specs=pl.BlockSpec(memory_space=pl.ANY),
        scratch_shapes=[pltpu.SemaphoreType.DMA((4,))] + [pltpu.SemaphoreType.DMA((4, n_slab))] * 2,
        compiler_params=pltpu.CompilerParams(
            collective_id=0, has_side_effects=True, vmem_limit_bytes=16 * 2**20
        ),
    )
    gathered = lax.cond(
        phonon_shift[0] > 0,
        gather,
        lambda *blocks: jnp.zeros((4, n_slab, orbitals, orbitals), jnp.float32),
        *own,
    )
    payload = pl.pallas_call(
        functools.partial(recursion_kernel, n_slab, n_energy),
        out_shape=jax.ShapeDtypeStruct((2, orbitals, orbitals), jnp.float32),
        in_specs=[pl.BlockSpec(memory_space=pltpu.VMEM)],
        out_specs=pl.BlockSpec(memory_space=pltpu.VMEM),
        scratch_shapes=[
            pltpu.VMEM((orbitals, orbitals), jnp.float32),
        ],
        compiler_params=pltpu.CompilerParams(vmem_limit_bytes=32 * 2**20),
    )(gathered)
    largest = min(2**OFFSET_BITS, n_energy // 2) - 1

    next_less, next_great = lax.switch(
        phonon_shift[0] - 1,
        [functools.partial(shifted_sum, offset) for offset in range(1, largest + 1)],
        occupation,
        payload,
    )
    return (next_less[None, None], next_great[None, None])


def solution(mesh):
    in_specs = (
        P("slab", None, None),
        P("slab", None, None),
        P("energy", "slab", None, None),
        P("energy", "slab", None, None),
        P(),
        P(),
    )
    out_specs = (P("energy", "slab", None, None), P("energy", "slab", None, None))
    return jax.shard_map(
        per_device, mesh=mesh, in_specs=in_specs, out_specs=out_specs, check_vma=False
    )
```
